32 devices in a mesh: row: 4 (over y, x), col: 8 (over z, core).
Axes of the slice: x: 2, y: 2, z: 4, core: 2. Of those that a mesh axis runs over, the one named last changes fastest.
Arguments:
- grad_out: bfloat16 [4096, 128], P(('row', 'col')), may hold values from -6 to 6
- pre_act: bfloat16 [4096, 128], P(('row', 'col')), may hold values from -6 to 6
- features: bfloat16 [4096, 128], P(('row', 'col')), may hold values from -6 to 6
- weight: bfloat16 [128, 128], replicated, may hold values from -0.5 to 0.5
- blocks: bfloat16 [4, 8, 8, 2, 128, 128], P('row', 'col'), may hold values from -0.125 to 0.125
- block_cols: int32 [4, 8, 8, 2], P('row', 'col'), may hold values from 0 to 3
- block_counts: int32 [4, 8, 8], P('row', 'col'), may hold values from 0 to 2, as said below
- order: int32 [4096], P(('row', 'col')), may hold values from 0 to 127, as said below
Outputs:
- grad_feat: bfloat16 [4096, 128], P(('row', 'col'))
- weight_grad: float32 [128, 128], replicated
The draws below stay inside these ranges and needn't reach their ends.
Inputs may be any that keep to these rules, and one draw needn't show every extreme that they name: `block_counts`: every device's slice has at least one row block with 2 nonzero blocks. `order`: each slab of 128 entries is a permutation of 0 to 127.
All inputs are finite; a program needn't handle non-finite values.
Results may differ from the reference program's by a relative error of at most 0.019.
Values may be sent and summed in bfloat16 or wider, within the bound.
No kernel may reach another device: no remote copies, remote signals or barrier semaphores. Data moves between devices by JAX's collectives and lax.ppermute only.
A program may use at most 64 MiB of HBM per device.

```python
import jax
import jax.numpy as jnp
from jax import lax

F = 128
B = 128
K = 2
BLK_DEV = 1
RB = 8
NCB = 4
NODES = 4096
N_ROW = 4
N_COL = 8


def draw_block_counts(key, part):
    key_level, key_trial, key_place = jax.random.split(jax.random.fold_in(key, 11), 3)
    level = jax.random.randint(key_level, (N_ROW, N_COL, 1, 1), 200, 1001)
    trials = jax.random.randint(key_trial, (N_ROW, N_COL, RB, K), 0, 1000)
    counts = jnp.sum((trials < level).astype(jnp.int32), axis=-1).astype(jnp.int32)
    place = jax.random.randint(key_place, (N_ROW, N_COL, 1), 0, RB)
    full_row = jnp.arange(RB, dtype=jnp.int32)[None, None, :] == place
    return jnp.where(full_row, K, counts).astype(jnp.int32)


def draw_order(key, part):
    slab_keys = jax.random.split(jax.random.fold_in(key, 23), N_ROW * N_COL)
    perms = jax.vmap(lambda single: jax.random.permutation(single, BLK_DEV * B))(slab_keys)
    return perms.reshape(-1).astype(jnp.int32)


def with_ends(result, own_key, least, high):
    longest = result.shape.index(max(result.shape))
    spots = []
    for shift in (0, 1):
        where = [jax.random.randint(jax.random.fold_in(own_key, axis), (), 0, length) for axis, length in enumerate(result.shape)]
        where[longest] = (where[longest] + shift) % result.shape[longest]
        spots.append(tuple(where))
    return result.at[spots[0]].set(least).at[spots[1]].set(high)


def shard_levels(key, shape, cuts, least, high):
    gain = 1.0
    for axis_at, blocks in cuts:
        steps = jax.random.uniform(jax.random.fold_in(jax.random.fold_in(key, 6), axis_at), (blocks,), jnp.float32, least / len(cuts), high / len(cuts))
        gain = gain * jnp.repeat(jnp.exp(steps), shape[axis_at] // blocks).reshape((-1,) + (1,) * (len(shape) - 1 - axis_at))
    return gain


def scatter_about(own_key, dims, width, reach, cuts=(), kind=jnp.bfloat16):
    drawn = jax.random.normal(own_key, dims, jnp.float32) * width
    if len(cuts) > 0:
        drawn = shard_levels(own_key, dims, cuts, -0.22, 0.18) * drawn
    return jnp.clip(drawn, min=-reach, max=reach).astype(kind)


def setup_inputs(seed: int = 0) -> dict:
    arg_keys = jax.random.split(jax.random.key(seed), 9)
    grad_out = scatter_about(arg_keys[0], (NODES, F), 1.0, 6.0, ((0, 32),))
    pre_act = scatter_about(arg_keys[1], (NODES, F), 1.0, 6.0, ((0, 32),))
    features = scatter_about(arg_keys[2], (NODES, F), 1.0, 6.0, ((0, 32),))
    weight = scatter_about(arg_keys[3], (F, F), F ** -0.5, 0.5)
    blocks = scatter_about(arg_keys[4], (N_ROW, N_COL, RB, K, B, B), (B * K * N_COL) ** -0.5, 0.125, ((0, 4), (1, 8)))
    block_cols = with_ends(jax.random.randint(arg_keys[5], (N_ROW, N_COL, RB, K), 0, NCB), jax.random.fold_in(arg_keys[5], 1), 0, NCB - 1).astype(jnp.int32)
    block_counts = draw_block_counts(jax.random.fold_in(arg_keys[8], 71), 0)
    order = draw_order(jax.random.fold_in(arg_keys[8], 71), 0)
    return dict(grad_out=grad_out, pre_act=pre_act, features=features, weight=weight, blocks=blocks, block_cols=block_cols, block_counts=block_counts, order=order)


def reference(grad_out, pre_act, features, weight, blocks, block_cols, block_counts, order):
    slab_rows = BLK_DEV * B
    positions = ((jnp.arange(NODES, dtype=jnp.int32) // slab_rows) * slab_rows + order).astype(jnp.int32)
    masked = jnp.where(pre_act > 0, grad_out, jnp.zeros_like(grad_out))
    masked_block = masked[positions]
    feat_block = features[positions]
    panels = masked_block.reshape(N_ROW, RB, B, F)

    def device_term(carry, device):
        row_id = device // N_COL
        col_id = device % N_COL
        block_vals = blocks[row_id, col_id].astype(jnp.float32)
        panel_rows = panels[row_id].astype(jnp.float32)
        products = jnp.einsum("ikrc,irf->ikcf", block_vals, panel_rows, precision=lax.Precision.HIGHEST)
        filled = jnp.arange(K, dtype=jnp.int32)[None, :] < block_counts[row_id, col_id][:, None]
        hits = block_cols[row_id, col_id][:, :, None] == jnp.arange(NCB, dtype=jnp.int32)[None, None, :]
        selector = jnp.where(hits & filled[:, :, None], 1.0, 0.0).astype(jnp.float32)
        partial_value = jnp.einsum("ikj,ikcf->jcf", selector, products, precision=lax.Precision.HIGHEST)
        rounded = lax.optimization_barrier(partial_value.astype(jnp.bfloat16)).astype(jnp.float32)
        carry = carry.at[:, col_id].add(rounded.reshape(N_ROW, BLK_DEV, B, F))
        return carry, None

    zero_sum = jnp.zeros((N_ROW, N_COL, BLK_DEV, B, F), jnp.float32)
    summed, _ = lax.scan(device_term, zero_sum, jnp.arange(N_ROW * N_COL, dtype=jnp.int32))
    owned = summed.reshape(NODES, F).astype(jnp.bfloat16)
    grad_block = jnp.dot(owned, weight.T, preferred_element_type=jnp.float32).astype(jnp.bfloat16)
    grad_feat = jnp.zeros_like(features).at[positions].set(grad_block)
    weight_grad = jnp.dot(feat_block.T, owned, preferred_element_type=jnp.float32) * (NODES ** -0.5)
    return grad_feat, weight_grad
```

```python
import functools

import jax
import jax.numpy as jnp
from jax import lax
from jax.experimental import pallas as pl
from jax.experimental.pallas import tpu as pltpu
from jax.sharding import PartitionSpec as P

F = 128
B = 128
K = 2
BF = jnp.bfloat16
F32 = jnp.float32
VMEM = pl.BlockSpec(memory_space=pltpu.VMEM)
SMEM = pl.BlockSpec(memory_space=pltpu.SMEM)


def swaps(size):
    return size & (size - 1) == 0


def target_of(index, step, size):
    return index ^ step if swaps(size) else (index + step) % size


def source_of(index, step, size):
    return index ^ step if swaps(size) else lax.rem(index + (size - step), size)


def dot(a, b, contract):
    return lax.dot_general(a, b, (contract, ((), ())), preferred_element_type=F32)


def call(body, outs, args, scalars=(), scratch=()):
    return pl.pallas_call(
        body,
        out_shape=outs,
        in_specs=[SMEM] * len(scalars) + [VMEM] * len(args),
        out_specs=[VMEM] * len(outs),
        scratch_shapes=list(scratch),
    )(*scalars, *args)


def spread(order_row):
    n = order_row.shape[1]
    return (lax.broadcasted_iota(jnp.int32, (n, n), 0) == order_row).astype(BF)


def first_kernel(grad_ref, pre_ref, feat_ref, order_ref, keep_ref, give_ref):
    core = lax.rem(lax.axis_index("col"), 2)
    place = spread(order_ref[...])
    grad = grad_ref[...]
    masked = jnp.where(pre_ref[...].astype(F32) > 0, grad.astype(F32), 0.0).astype(BF)
    masked = dot(place, masked, ((0,), (0,))).astype(BF)
    feat = dot(place, feat_ref[...], ((0,), (0,))).astype(BF)
    even = core == 0
    keep_ref[...] = jnp.where(even, masked, feat)
    give_ref[...] = jnp.where(even, feat, masked)


def product_kernel(rows, depth, *refs):
    steps = max(rows, depth)
    cols_ref, counts_ref = refs[0], refs[1]
    blocks_ref = refs[2]
    own, other = refs[3 : 3 + steps], refs[3 + steps : 3 + 2 * steps]
    outs = refs[3 + 2 * steps : -1]
    total = refs[-1]
    r = lax.axis_index("row")
    c = lax.axis_index("col")
    z, even = lax.div(c, 2), lax.rem(c, 2) == 0
    total[...] = jnp.zeros_like(total)
    for step in range(depth):
        pair = jnp.where(even, own[step][...], other[step][...])
        chip = source_of(z, step, depth)
        for core in range(2):
            i = 2 * chip + core
            panel = pair[core * B : (core + 1) * B]
            for k in range(K):
                j = jnp.where(k < counts_ref[0, 0, i], cols_ref[0, 0, i, k], rows)
                total[j] += dot(blocks_ref[0, 0, i, k], panel, ((0,), (0,)))
    terms = [total[source_of(r, step, rows)].astype(BF) for step in range(rows)]
    weight = jnp.zeros((F, F), F32)
    for step in range(rows):
        feat = jnp.where(even, other[step][B : 2 * B], own[step][0:B])
        weight += dot(feat, terms[step], ((0,), (0,)))
    weight = weight.astype(BF)
    outs[0][0:B] = terms[0]
    outs[0][B : 2 * B] = weight
    for step in range(1, rows):
        out = terms[step] if swaps(rows) else terms[rows - step]
        outs[step][0:B] = out
        outs[step][B : 2 * B] = weight


def sum_in_order(values, index, size):
    values = [v.astype(F32) for v in values]
    if swaps(size):
        while len(values) > 1:
            values = [a + b for a, b in zip(values[0::2], values[1::2])]
        return values[0]
    places = jnp.stack([source_of(index, step, size) for step in range(size)])
    held = jnp.zeros((size,) + values[0].shape, F32).at[places].set(jnp.stack(values))
    return functools.reduce(lambda a, b: a + b, [held[i] for i in range(size)])


def feature_kernel(count, order_ref, weight_ref, *refs):
    terms, out_ref = refs[:count], refs[count]
    total = terms[0][0:B].astype(F32)
    for term in terms[1:]:
        total += term[0:B].astype(F32)
    grad = dot(total.astype(BF), weight_ref[...], ((1,), (1,))).astype(BF)
    out_ref[...] = dot(spread(order_ref[...]), grad, ((1,), (0,))).astype(BF)


def shards(grad_out, pre_act, features, weight, blocks, block_cols, block_counts, order):
    slab_rows = grad_out.shape[0]
    rows = lax.axis_size("row")
    cols = lax.axis_size("col")
    depth = cols // 2
    axes = ("row", "col")
    r, z = lax.axis_index("row"), lax.div(lax.axis_index("col"), 2)
    order_row = order.reshape(1, slab_rows)
    slab = jax.ShapeDtypeStruct((B, F), BF)
    pair = jax.ShapeDtypeStruct((2 * B, F), BF)

    def across(value):
        return lax.ppermute(value, "col", [(i, i ^ 1) for i in range(cols)])

    def along_row(value, step):
        return lax.ppermute(value, "row", [(i, target_of(i, step, rows)) for i in range(rows)])

    def along_depth(value, step):
        pairs = [(i, 2 * target_of(i // 2, step, depth) + i % 2) for i in range(cols)]
        return lax.ppermute(value, "col", pairs)

    def both(value, step):
        pairs = []
        for i in range(rows):
            for j in range(depth):
                if step < depth:
                    pairs.append((i * cols + 2 * j, i * cols + 2 * target_of(j, step, depth)))
                if step < rows:
                    pairs.append((i * cols + 2 * j + 1, target_of(i, step, rows) * cols + 2 * j + 1))
        return lax.ppermute(value, axes, pairs)

    keep, give = call(first_kernel, [slab, slab], (grad_out, pre_act, features, order_row))
    message = jnp.concatenate([keep, across(give)], axis=0)
    steps = max(rows, depth)
    own = [message] + [both(message, step) for step in reversed(range(1, steps))][::-1]
    other = [across(value) for value in own]
    out = call(
        functools.partial(product_kernel, rows, depth),
        [pair] * rows,
        (blocks, *own, *other),
        scalars=(block_cols, block_counts),
        scratch=[pltpu.VMEM((rows + 1, B, F), F32)],
    )
    terms = [out[0]] + [along_row(out[step], step) for step in range(1, rows)]
    total = sum_in_order([term[B:] for term in terms], r, rows)
    total = (total + across(total)).astype(BF)
    (grad_feat,) = call(functools.partial(feature_kernel, rows), [slab], (order_row, weight, *terms))
    totals = [total] + [along_depth(total, step) for step in range(1, depth)]
    summed = sum_in_order(totals, z, depth)
    return grad_feat, summed * (slab_rows * rows * cols) ** (-0.5)


def solution(mesh):
    placed = (
        P(("row", "col"), None),
        P(("row", "col"), None),
        P(("row", "col"), None),
        P(),
        P("row", "col", None, None, None, None),
        P("row", "col", None, None),
        P("row", "col", None),
        P(("row", "col")),
    )
    return jax.shard_map(
        shards,
        mesh=mesh,
        in_specs=placed,
        out_specs=(P(("row", "col"), None), P()),
        check_vma=False,
    )
```

```python
import functools

import jax
import jax.numpy as jnp
from jax import lax
from jax.experimental import pallas as pl
from jax.experimental.pallas import tpu as pltpu
from jax.sharding import PartitionSpec as P

F = 128
B = 128
K = 2
BF = jnp.bfloat16
F32 = jnp.float32


def swaps(size):
    return size & (size - 1) == 0


def target_of(index, step, size):
    return index ^ step if swaps(size) else (index + step) % size


def source_of(index, step, size):
    return index ^ step if swaps(size) else lax.rem(index + (size - step), size)


def dot(a, b, contract):
    return lax.dot_general(a, b, (contract, ((), ())), preferred_element_type=F32)


def call(body, outs, args, spaces, out_spaces=None, scratch=(), limit=4 << 20):
    return pl.pallas_call(
        body,
        out_shape=outs,
        in_specs=[pl.BlockSpec(memory_space=space) for space in spaces],
        out_specs=[pl.BlockSpec(memory_space=pltpu.VMEM)] * len(outs),
        scratch_shapes=list(scratch),
        compiler_params=pltpu.CompilerParams(vmem_limit_bytes=limit),
    )(*args)


def spread(order_row):
    n = order_row.shape[1]
    return (lax.broadcasted_iota(jnp.int32, (n, n), 0) == order_row).astype(BF)


def first_kernel(order_ref, keep_ref, give_ref, keep_out, give_out):
    place = spread(order_ref[...])
    keep_out[...] = dot(place, keep_ref[...], ((0,), (0,))).astype(BF)
    give_out[...] = dot(place, give_ref[...], ((0,), (0,))).astype(BF)


def row_steps(rows):
    return list(zip([1, 2, *range(3, rows)], [2, 1, *range(3, rows)]))


def product_kernel(rows, depth, *refs):
    steps = max(rows, depth)
    cols_ref, blocks_ref = refs[:2]
    own, other = refs[2 : 2 + steps], refs[2 + steps : 2 + 2 * steps]
    term_ref, weight_ref = refs[2 + 2 * steps : 4 + 2 * steps]
    outs = refs[4 + 2 * steps : -1]
    total = refs[-1]
    r = lax.axis_index("row")
    c = lax.axis_index("col")
    z, even = lax.div(c, 2), lax.rem(c, 2) == 0
    total[...] = jnp.zeros_like(total)
    for step in range(depth):
        pair = jnp.where(even, own[step][...], other[step][...])
        chip = source_of(z, step, depth)
        for core in range(2):
            i = 2 * chip + core
            panel = pair[core * B : (core + 1) * B]
            for k in range(K):
                total[cols_ref[k, i]] += dot(blocks_ref[i, k], panel, ((0,), (0,)))
    terms = [total[source_of(r, step, rows)].astype(BF) for step in range(rows)]
    weight = jnp.zeros((F, F), F32)
    for step in range(rows):
        feat = jnp.where(even, other[step][B : 2 * B], own[step][0:B])
        weight += dot(feat, terms[step], ((0,), (0,)))
    term_ref[...] = terms[0]
    weight_ref[...] = weight
    sent = terms if swaps(rows) else [terms[-step] for step in range(rows)]
    for out, (first, second) in zip(outs, row_steps(rows)):
        out[0:B] = jnp.where(even, sent[first], sent[second])


def sum_in_order(values, index, size):
    values = [v.astype(F32) for v in values]
    if swaps(size):
        while len(values) > 1:
            values = [a + b for a, b in zip(values[0::2], values[1::2])]
        return values[0]
    places = jnp.stack([source_of(index, step, size) for step in range(size)])
    held = jnp.zeros((size,) + values[0].shape, F32).at[places].set(jnp.stack(values))
    return functools.reduce(lambda a, b: a + b, [held[i] for i in range(size)])


def feature_kernel(count, order_ref, weight_ref, *refs):
    terms, out_ref = refs[:count], refs[count]
    total = terms[0][0:B].astype(F32)
    for term in terms[1:]:
        total += term[0:B].astype(F32)
    grad = dot(total.astype(BF), weight_ref[...], ((1,), (1,))).astype(BF)
    out_ref[...] = dot(spread(order_ref[...]), grad, ((1,), (0,))).astype(BF)


def shards(grad_out, pre_act, features, weight, blocks, block_cols, block_counts, order):
    slab_rows = grad_out.shape[0]
    rows = lax.axis_size("row")
    cols = lax.axis_size("col")
    depth = cols // 2
    axes = ("row", "col")
    r, c = lax.axis_index("row"), lax.axis_index("col")
    z, even = lax.div(c, 2), lax.rem(c, 2) == 0
    order_row = order.reshape(1, slab_rows)
    slab = jax.ShapeDtypeStruct((B, F), BF)
    pair = jax.ShapeDtypeStruct((2 * B, F), BF)
    limit = (4 << 20) + 8 * blocks.size

    def across(value):
        return lax.ppermute(value, "col", [(i, i ^ 1) for i in range(cols)])

    def move(value, row_of, depth_of):
        pairs = []
        for i in range(rows):
            for j in range(depth):
                for core in range(2):
                    a, b = row_of(i, core), depth_of(j, core)
                    if a is not None and b is not None:
                        pairs.append((i * cols + 2 * j + core, a * cols + 2 * b + core))
        return lax.ppermute(value, axes, pairs)

    def along_row(value, steps):
        return move(value, lambda i, core: target_of(i, steps[core], rows), lambda j, core: j)

    def along_depth(value, steps):
        return move(value, lambda i, core: i, lambda j, core: target_of(j, steps[core], depth))

    def both(value, step):
        return move(
            value,
            lambda i, core: i if core == 0 else target_of(i, step, rows) if step < rows else None,
            lambda j, core: j if core == 1 else target_of(j, step, depth) if step < depth else None,
        )

    masked = jnp.where(pre_act > 0, grad_out, jnp.zeros_like(grad_out))
    keep, give = jnp.where(even, masked, features), jnp.where(even, features, masked)
    keep, give = call(first_kernel, [slab, slab], (order_row, keep, give), [pltpu.VMEM] * 3)
    filled = jnp.arange(K, dtype=jnp.int32)[None, :] < block_counts[0, 0][:, None]
    blocks = jnp.where(filled[:, :, None, None], blocks[0, 0], jnp.zeros((), BF))
    message = jnp.concatenate([keep, across(give)], axis=0)
    steps = max(rows, depth)
    own = [message] + [both(message, step) for step in reversed(range(1, steps))][::-1]
    other = [across(value) for value in own]
    term, weight_term, *messages = call(
        functools.partial(product_kernel, rows, depth),
        [slab, jax.ShapeDtypeStruct((F, F), F32), slab] + [pair] * (rows - 2),
        (block_cols[0, 0].T, blocks, *own, *other),
        [pltpu.SMEM] + [pltpu.VMEM] * (1 + 2 * steps),
        scratch=[pltpu.VMEM((rows, B, F), F32)],
        limit=limit,
    )
    chip_weight = (weight_term + across(weight_term)).astype(BF)
    plan = row_steps(rows)
    terms = [along_row(messages[0], plan[0])]
    terms += [along_row(m.at[B:].set(chip_weight), plan[i + 1]) for i, m in enumerate(messages[1:])]
    (grad_feat,) = call(
        functools.partial(feature_kernel, rows), [slab], (order_row, weight, term, *terms), [pltpu.VMEM] * (2 + rows)
    )
    terms = list(lax.optimization_barrier(tuple(terms)))
    mine = terms[1][B:]
    swapped = across(mine)
    weights = [chip_weight, jnp.where(even, swapped, mine), jnp.where(even, mine, swapped)] + [t[B:] for t in terms[2:]]
    row_weight = sum_in_order(weights, r, rows).astype(BF)
    mine = along_depth(row_weight, (1, 2))
    rest = [along_depth(row_weight, (step, step)) for step in range(3, depth)]
    swapped = across(mine)
    weights = [row_weight, jnp.where(even, mine, swapped), jnp.where(even, swapped, mine)] + rest
    summed = sum_in_order(weights, z, depth)
    return grad_feat, summed * (slab_rows * rows * cols) ** (-0.5)


def solution(mesh):
    placed = (
        P(("row", "col"), None),
        P(("row", "col"), None),
        P(("row", "col"), None),
        P(),
        P("row", "col", None, None, None, None),
        P("row", "col", None, None),
        P("row", "col", None),
        P(("row", "col")),
    )
    return jax.shard_map(
        shards,
        mesh=mesh,
        in_specs=placed,
        out_specs=(P(("row", "col"), None), P()),
        check_vma=False,
    )
```

```python
import functools

import jax
import jax.numpy as jnp
from jax import lax
from jax.experimental import pallas as pl
from jax.experimental.pallas import tpu as pltpu
from jax.sharding import PartitionSpec as P

F = 128
B = 128
K = 2
BF = jnp.bfloat16
F32 = jnp.float32


def swaps(size):
    return size & (size - 1) == 0


def target_of(index, step, size):
    return index ^ step if swaps(size) else (index + step) % size


def source_of(index, step, size):
    return index ^ step if swaps(size) else lax.rem(index + (size - step), size)


def far_steps(size):
    return [0, 1, *range(size - 1, 1, -1)]


def dot(a, b, contract):
    return lax.dot_general(a, b, (contract, ((), ())), preferred_element_type=F32)


def call(body, outs, args, spaces, out_spaces=None, scratch=(), limit=4 << 20):
    return pl.pallas_call(
        body,
        out_shape=outs,
        in_specs=[pl.BlockSpec(memory_space=space) for space in spaces],
        out_specs=[pl.BlockSpec(memory_space=pltpu.VMEM)] * len(outs),
        scratch_shapes=list(scratch),
        compiler_params=pltpu.CompilerParams(vmem_limit_bytes=limit),
    )(*args)


def spread(order_row):
    n = order_row.shape[1]
    return (lax.broadcasted_iota(jnp.int32, (n, n), 0) == order_row).astype(BF)


def first_kernel(order_ref, keep_ref, give_ref, keep_out, give_out):
    place = spread(order_ref[...])
    keep_out[...] = dot(place, keep_ref[...], ((0,), (0,))).astype(BF)
    give_out[...] = dot(place, give_ref[...], ((0,), (0,))).astype(BF)


def product_kernel(rows, depth, *refs):
    steps = max(rows, depth)
    cols_ref, blocks_ref = refs[:2]
    own, other = refs[2 : 2 + steps], refs[2 + steps : 2 + 2 * steps]
    term_ref, weight_ref = refs[2 + 2 * steps : 4 + 2 * steps]
    outs = refs[4 + 2 * steps : -1]
    total = refs[-1]
    r = lax.axis_index("row")
    c = lax.axis_index("col")
    z, even = lax.div(c, 2), lax.rem(c, 2) == 0
    total[...] = jnp.zeros_like(total)
    for slot, step in enumerate(far_steps(depth)):
        pair = jnp.where(even, own[slot][...], other[slot][...])
        chip = source_of(z, step, depth)
        for core in range(2):
            i = 2 * chip + core
            panel = pair[core * B : (core + 1) * B]
            for k in range(K):
                total[cols_ref[k, i]] += dot(blocks_ref[i, k], panel, ((0,), (0,)))
    terms = [total[source_of(r, step, rows)].astype(BF) for step in range(rows)]
    weight = jnp.zeros((F, F), F32)
    for slot, step in enumerate(far_steps(rows)):
        feat = jnp.where(even, other[slot][B : 2 * B], own[slot][0:B])
        weight += dot(feat, terms[step], ((0,), (0,)))
    term_ref[...] = terms[0]
    weight_ref[...] = weight
    for step, out in zip(far_steps(rows)[1:], outs):
        out[0:B] = terms[step] if swaps(rows) else terms[rows - step]


def sum_in_order(values, index, size):
    values = [v.astype(F32) for v in values]
    if swaps(size):
        while len(values) > 1:
            values = [a + b for a, b in zip(values[0::2], values[1::2])]
        return values[0]
    places = jnp.stack([source_of(index, step, size) for step in range(size)])
    held = jnp.zeros((size,) + values[0].shape, F32).at[places].set(jnp.stack(values))
    return functools.reduce(lambda a, b: a + b, [held[i] for i in range(size)])


def feature_kernel(count, order_ref, weight_ref, *refs):
    terms, out_ref = refs[:count], refs[count]
    total = terms[0][0:B].astype(F32)
    for term in terms[1:]:
        total += term[0:B].astype(F32)
    grad = dot(total.astype(BF), weight_ref[...], ((1,), (1,))).astype(BF)
    out_ref[...] = dot(spread(order_ref[...]), grad, ((1,), (0,))).astype(BF)


def shards(grad_out, pre_act, features, weight, blocks, block_cols, block_counts, order):
    slab_rows = grad_out.shape[0]
    rows = lax.axis_size("row")
    cols = lax.axis_size("col")
    depth = cols // 2
    axes = ("row", "col")
    r, c = lax.axis_index("row"), lax.axis_index("col")
    z, even = lax.div(c, 2), lax.rem(c, 2) == 0
    order_row = order.reshape(1, slab_rows)
    slab = jax.ShapeDtypeStruct((B, F), BF)
    pair = jax.ShapeDtypeStruct((2 * B, F), BF)
    limit = (4 << 20) + 8 * blocks.size

    def across(value):
        return lax.ppermute(value, "col", [(i, i ^ 1) for i in range(cols)])

    def move(value, row_of, depth_of):
        pairs = []
        for i in range(rows):
            for j in range(depth):
                for core in range(2):
                    a, b = row_of(i, core), depth_of(j, core)
                    if a is not None and b is not None:
                        pairs.append((i * cols + 2 * j + core, a * cols + 2 * b + core))
        return lax.ppermute(value, axes, pairs)

    def along_row(value, steps):
        return move(value, lambda i, core: target_of(i, steps[core], rows), lambda j, core: j)

    def along_depth(value, steps):
        return move(value, lambda i, core: i, lambda j, core: target_of(j, steps[core], depth))

    def both(value, slot):
        def row_of(i, core):
            return i if core == 0 else target_of(i, far_steps(rows)[slot], rows) if slot < rows else None

        def depth_of(j, core):
            return j if core == 1 else target_of(j, far_steps(depth)[slot], depth) if slot < depth else None

        return move(value, row_of, depth_of)

    masked = jnp.where(pre_act > 0, grad_out, jnp.zeros_like(grad_out))
    keep, give = jnp.where(even, masked, features), jnp.where(even, features, masked)
    keep, give = call(first_kernel, [slab, slab], (order_row, keep, give), [pltpu.VMEM] * 3)
    message = jnp.concatenate([keep, across(give)], axis=0)
    message, counts = lax.optimization_barrier((message, block_counts))
    filled = jnp.arange(K, dtype=jnp.int32)[:, None] < counts[0, 0][None, :]
    targets = jnp.where(filled, block_cols[0, 0].T, 0)
    blocks = jnp.where(filled.T[:, :, None, None], blocks[0, 0], jnp.zeros((), BF))
    steps = max(rows, depth)
    own = [message] + [both(message, slot) for slot in range(1, steps)]
    other = [across(value) for value in own]
    term, weight_term, *messages = call(
        functools.partial(product_kernel, rows, depth),
        [slab, jax.ShapeDtypeStruct((F, F), F32)] + [pair] * (rows - 1),
        (targets, blocks, *own, *other),
        [pltpu.SMEM] + [pltpu.VMEM] * (1 + 2 * steps),
        scratch=[pltpu.VMEM((rows, B, F), F32)],
        limit=limit,
    )
    chip_weight = (weight_term + across(weight_term)).astype(BF)
    row_plan = far_steps(rows)[1:]
    terms = [along_row(m.at[B:].set(chip_weight), (step, step)) for step, m in zip(row_plan, messages)]
    (grad_feat,) = call(
        functools.partial(feature_kernel, rows), [slab], (order_row, weight, term, *terms), [pltpu.VMEM] * (2 + rows)
    )
    by_step = dict(zip(row_plan, terms))
    weights = [chip_weight] + [by_step[step][B:] for step in range(1, rows)]
    row_weight = sum_in_order(weights, r, rows).astype(BF)
    mine = along_depth(row_weight, (1, 2))
    rest = [along_depth(row_weight, (step, step)) for step in range(3, depth)]
    swapped = across(mine)
    weights = [row_weight, jnp.where(even, mine, swapped), jnp.where(even, swapped, mine)] + rest
    summed = sum_in_order(weights, z, depth)
    return grad_feat, summed * (slab_rows * rows * cols) ** (-0.5)


def solution(mesh):
    placed = (
        P(("row", "col"), None),
        P(("row", "col"), None),
        P(("row", "col"), None),
        P(),
        P("row", "col", None, None, None, None),
        P("row", "col", None, None),
        P("row", "col", None),
        P(("row", "col")),
    )
    return jax.shard_map(
        shards,
        mesh=mesh,
        in_specs=placed,
        out_specs=(P(("row", "col"), None), P()),
        check_vma=False,
    )
```

```python
import functools

import jax
import jax.numpy as jnp
from jax import lax
from jax.experimental import pallas as pl
from jax.experimental.pallas import tpu as pltpu
from jax.sharding import PartitionSpec as P

F = 128
B = 128
K = 2
BF = jnp.bfloat16
F32 = jnp.float32


def swaps(size):
    return size & (size - 1) == 0


def target_of(index, step, size):
    return index ^ step if swaps(size) else (index + step) % size


def source_of(index, step, size):
    return index ^ step if swaps(size) else lax.rem(index + (size - step), size)


def far_steps(size):
    return [0, 1, *range(size - 1, 1, -1)]


def dot(a, b, contract):
    return lax.dot_general(a, b, (contract, ((), ())), preferred_element_type=F32)


def call(body, outs, args, spaces, scratch=(), limit=4 << 20):
    return pl.pallas_call(
        body,
        out_shape=outs,
        in_specs=[pl.BlockSpec(memory_space=space) for space in spaces],
        out_specs=[pl.BlockSpec(memory_space=pltpu.VMEM)] * len(outs),
        scratch_shapes=list(scratch),
        compiler_params=pltpu.CompilerParams(vmem_limit_bytes=limit),
    )(*args)


def spread(order_row):
    n = order_row.shape[1]
    return (lax.broadcasted_iota(jnp.int32, (n, n), 0) == order_row).astype(BF)


def first_kernel(order_ref, keep_ref, give_ref, keep_out, give_out):
    place = spread(order_ref[...])
    keep_out[...] = dot(place, keep_ref[...], ((0,), (0,))).astype(BF)
    give_out[...] = dot(place, give_ref[...], ((0,), (0,))).astype(BF)


def row_steps(rows):
    return list(zip([1, 2, *range(3, rows)], [2, 1, *range(3, rows)]))


def product_kernel(rows, depth, *refs):
    steps = max(rows, depth)
    targets_vmem, blocks_ref = refs[:2]
    own, other = refs[2 : 2 + steps], refs[2 + steps : 2 + 2 * steps]
    term_ref, weight_ref = refs[2 + 2 * steps : 4 + 2 * steps]
    outs = refs[4 + 2 * steps : -4]
    total, products, targets_ref, sem = refs[-4:]
    fetch = pltpu.make_async_copy(targets_vmem, targets_ref, sem)
    fetch.start()
    r = lax.axis_index("row")
    c = lax.axis_index("col")
    z, even = lax.div(c, 2), lax.rem(c, 2) == 0
    for slot, step in enumerate(far_steps(depth)):
        pair = jnp.where(even, own[slot][...], other[slot][...])
        chip = source_of(z, step, depth)
        for core in range(2):
            panel = pair[core * B : (core + 1) * B]
            for k in range(K):
                place = (2 * slot + core) * K + k
                products[place] = dot(blocks_ref[2 * chip + core, k], panel, ((0,), (0,)))
    total[...] = jnp.zeros_like(total)
    fetch.wait()
    for slot, step in enumerate(far_steps(depth)):
        chip = source_of(z, step, depth)
        for core in range(2):
            for k in range(K):
                total[targets_ref[k, 2 * chip + core]] += products[(2 * slot + core) * K + k]
    terms = [total[source_of(r, step, rows)].astype(BF) for step in range(rows)]
    weight = jnp.zeros((F, F), F32)
    for slot, step in enumerate(far_steps(rows)):
        feat = jnp.where(even, other[slot][B : 2 * B], own[slot][0:B])
        weight += dot(feat, terms[step], ((0,), (0,)))
    term_ref[...] = terms[0]
    weight_ref[...] = weight
    sent = terms if swaps(rows) else [terms[-step] for step in range(rows)]
    for out, (first, second) in zip(outs, row_steps(rows)):
        out[0:B] = jnp.where(even, sent[first], sent[second])
    outs[0][B : 2 * B] = jnp.zeros((B, F), BF)


def sum_in_order(values, index, size):
    values = [v.astype(F32) for v in values]
    if swaps(size):
        while len(values) > 1:
            values = [a + b for a, b in zip(values[0::2], values[1::2])]
        return values[0]
    places = jnp.stack([source_of(index, step, size) for step in range(size)])
    held = jnp.zeros((size,) + values[0].shape, F32).at[places].set(jnp.stack(values))
    return functools.reduce(lambda a, b: a + b, [held[i] for i in range(size)])


def feature_kernel(count, order_ref, weight_ref, *refs):
    terms, out_ref = refs[:count], refs[count]
    total = terms[0][0:B].astype(F32)
    for term in terms[1:]:
        total += term[0:B].astype(F32)
    grad = dot(total.astype(BF), weight_ref[...], ((1,), (1,))).astype(BF)
    out_ref[...] = dot(spread(order_ref[...]), grad, ((1,), (0,))).astype(BF)


def shards(grad_out, pre_act, features, weight, blocks, block_cols, block_counts, order):
    slab_rows = grad_out.shape[0]
    rows = lax.axis_size("row")
    cols = lax.axis_size("col")
    depth = cols // 2
    axes = ("row", "col")
    r, c = lax.axis_index("row"), lax.axis_index("col")
    z, even = lax.div(c, 2), lax.rem(c, 2) == 0
    order_row = order.reshape(1, slab_rows)
    slab = jax.ShapeDtypeStruct((B, F), BF)
    pair = jax.ShapeDtypeStruct((2 * B, F), BF)
    limit = (4 << 20) + 8 * blocks.size

    def across(value):
        return lax.ppermute(value, "col", [(i, i ^ 1) for i in range(cols)])

    def move(value, row_of, depth_of):
        pairs = []
        for i in range(rows):
            for j in range(depth):
                for core in range(2):
                    a, b = row_of(i, core), depth_of(j, core)
                    if a is not None and b is not None:
                        pairs.append((i * cols + 2 * j + core, a * cols + 2 * b + core))
        return lax.ppermute(value, axes, pairs)

    def along_row(value, steps):
        return move(value, lambda i, core: target_of(i, steps[core], rows), lambda j, core: j)

    def along_depth(value, steps):
        return move(value, lambda i, core: i, lambda j, core: target_of(j, steps[core], depth))

    def both(value, slot):
        def row_of(i, core):
            return i if core == 0 else target_of(i, far_steps(rows)[slot], rows) if slot < rows else None

        def depth_of(j, core):
            return j if core == 1 else target_of(j, far_steps(depth)[slot], depth) if slot < depth else None

        return move(value, row_of, depth_of)

    masked = jnp.where(pre_act > 0, grad_out, jnp.zeros_like(grad_out))
    keep, give = jnp.where(even, masked, features), jnp.where(even, features, masked)
    keep, give = call(first_kernel, [slab, slab], (order_row, keep, give), [pltpu.VMEM] * 3)
    message = jnp.concatenate([keep, across(give)], axis=0)
    message, counts = lax.optimization_barrier((message, block_counts))
    filled = jnp.arange(K, dtype=jnp.int32)[:, None] < counts[0, 0][None, :]
    targets = jnp.where(filled, block_cols[0, 0].T, 0)
    blocks = jnp.where(filled.T[:, :, None, None], blocks[0, 0], jnp.zeros((), BF))
    steps = max(rows, depth)
    own = [message] + [both(message, slot) for slot in range(1, steps)]
    held, targets, blocks = lax.optimization_barrier((message, targets, blocks))
    other = [across(value) for value in (held, *own[1:])]
    term, weight_term, *messages = call(
        functools.partial(product_kernel, rows, depth),
        [slab, jax.ShapeDtypeStruct((F, F), F32), pair] + [pair] * (rows - 2),
        (targets, blocks, *own, *other),
        [pltpu.VMEM] * (2 + 2 * steps),
        scratch=[
            pltpu.VMEM((rows, B, F), F32),
            pltpu.VMEM((cols * K, B, F), F32),
            pltpu.SMEM(targets.shape, jnp.int32),
            pltpu.SemaphoreType.DMA,
        ],
        limit=limit,
    )
    chip_weight = (weight_term + across(weight_term)).astype(BF)
    plan = row_steps(rows)
    terms = [along_row(messages[0], plan[0])]
    terms += [along_row(m.at[B:].set(chip_weight), plan[i]) for i, m in enumerate(messages) if i > 0]
    (grad_feat,) = call(
        functools.partial(feature_kernel, rows), [slab], (order_row, weight, term, *terms), [pltpu.VMEM] * (rows + 2)
    )
    mine = terms[1][B:]
    swapped = across(mine)
    weights = [chip_weight, jnp.where(even, swapped, mine), jnp.where(even, mine, swapped)] + [t[B:] for t in terms[2:]]
    row_weight = sum_in_order(weights, r, rows).astype(BF)
    mine = along_depth(row_weight, (1, 2))
    rest = [along_depth(row_weight, (step, step)) for step in range(3, depth)]
    swapped = across(mine)
    weights = [row_weight, jnp.where(even, mine, swapped), jnp.where(even, swapped, mine)] + rest
    summed = sum_in_order(weights, z, depth)
    return grad_feat, summed * (slab_rows * rows * cols) ** (-0.5)


def solution(mesh):
    placed = (
        P(("row", "col"), None),
        P(("row", "col"), None),
        P(("row", "col"), None),
        P(),
        P("row", "col", None, None, None, None),
        P("row", "col", None, None),
        P("row", "col", None),
        P(("row", "col")),
    )
    return jax.shard_map(
        shards,
        mesh=mesh,
        in_specs=placed,
        out_specs=(P(("row", "col"), None), P()),
        check_vma=False,
    )
```

```python
import functools

import jax
import jax.numpy as jnp
import numpy as np
from jax import lax
from jax.experimental import pallas as pl
from jax.experimental.pallas import tpu as pltpu
from jax.sharding import PartitionSpec as P

F = 128
B = 128
K = 2
BF = jnp.bfloat16
F32 = jnp.float32


def swaps(size):
    return size & (size - 1) == 0


def target_of(index, step, size):
    return index ^ step if swaps(size) else (index + step) % size


def source_of(index, step, size):
    return index ^ step if swaps(size) else lax.rem(index + (size - step), size)


def far_steps(size):
    return [0, 1, *range(size - 1, 1, -1)]


def dot(a, b, contract):
    return lax.dot_general(a, b, (contract, ((), ())), preferred_element_type=F32)


def call(body, outs, args, spaces, scratch=(), limit=4 << 20):
    return pl.pallas_call(
        body,
        out_shape=outs,
        in_specs=[pl.BlockSpec(memory_space=space) for space in spaces],
        out_specs=[pl.BlockSpec(memory_space=pltpu.VMEM)] * len(outs),
        scratch_shapes=list(scratch),
        compiler_params=pltpu.CompilerParams(vmem_limit_bytes=limit),
    )(*args)


def row_steps(rows):
    return list(zip([1, 2, *range(3, rows)], [2, 1, *range(3, rows)]))


def product_kernel(rows, depth, *refs):
    steps = max(rows, depth)
    targets_vmem, blocks_ref = refs[:2]
    own, other = refs[2 : 2 + steps], refs[2 + steps : 2 + 2 * steps]
    term_ref, weight_ref = refs[2 + 2 * steps : 4 + 2 * steps]
    outs = refs[4 + 2 * steps : -4]
    total, products, targets_ref, sem = refs[-4:]
    fetch = pltpu.make_async_copy(targets_vmem, targets_ref, sem)
    fetch.start()
    r = lax.axis_index("row")
    c = lax.axis_index("col")
    z, even = lax.div(c, 2), lax.rem(c, 2) == 0
    for slot, step in enumerate(far_steps(depth)):
        pair = jnp.where(even, own[slot][...], other[slot][...])
        chip = source_of(z, step, depth)
        for core in range(2):
            panel = pair[core * B : (core + 1) * B]
            for k in range(K):
                place = (2 * slot + core) * K + k
                products[place] = dot(blocks_ref[2 * chip + core, k], panel, ((0,), (0,)))
    total[...] = jnp.zeros_like(total)
    fetch.wait()
    for slot, step in enumerate(far_steps(depth)):
        chip = source_of(z, step, depth)
        for core in range(2):
            for k in range(K):
                total[targets_ref[k, 2 * chip + core]] += products[(2 * slot + core) * K + k]
    terms = [total[source_of(r, step, rows)].astype(BF) for step in range(rows)]
    weight = jnp.zeros((F, F), F32)
    for slot, step in enumerate(far_steps(rows)):
        feat = jnp.where(even, other[slot][B : 2 * B], own[slot][0:B])
        weight += dot(feat, terms[step], ((0,), (0,)))
    term_ref[...] = terms[0]
    weight_ref[...] = weight
    sent = terms if swaps(rows) else [terms[-step] for step in range(rows)]
    for out, (first, second) in zip(outs, row_steps(rows)):
        out[0:B] = jnp.where(even, sent[first], sent[second])
    outs[0][B : 2 * B] = jnp.zeros((B, F), BF)


def sum_in_order(values, index, size):
    values = [v.astype(F32) for v in values]
    if swaps(size):
        while len(values) > 1:
            values = [a + b for a, b in zip(values[0::2], values[1::2])]
        return values[0]
    places = jnp.stack([source_of(index, step, size) for step in range(size)])
    held = jnp.zeros((size,) + values[0].shape, F32).at[places].set(jnp.stack(values))
    return functools.reduce(lambda a, b: a + b, [held[i] for i in range(size)])


def feature_kernel(count, place_ref, weight_ref, *refs):
    terms, out_ref = refs[:count], refs[count]
    total = terms[0][0:B].astype(F32)
    for term in terms[1:]:
        total += term[0:B].astype(F32)
    grad = dot(total.astype(BF), weight_ref[...], ((1,), (1,))).astype(BF)
    out_ref[...] = dot(place_ref[...], grad, ((0,), (0,))).astype(BF)


def shards(grad_out, pre_act, features, weight, blocks, block_cols, block_counts, order):
    slab_rows = grad_out.shape[0]
    rows = lax.axis_size("row")
    cols = lax.axis_size("col")
    depth = cols // 2
    axes = ("row", "col")
    r, c = lax.axis_index("row"), lax.axis_index("col")
    z, even = lax.div(c, 2), lax.rem(c, 2) == 0
    slab = jax.ShapeDtypeStruct((B, F), BF)
    pair = jax.ShapeDtypeStruct((2 * B, F), BF)
    limit = (4 << 20) + 8 * blocks.size

    def across(value):
        return lax.ppermute(value, "col", [(i, i ^ 1) for i in range(cols)])

    def move(value, row_of, depth_of):
        pairs = []
        for i in range(rows):
            for j in range(depth):
                for core in range(2):
                    a, b = row_of(i, core), depth_of(j, core)
                    if a is not None and b is not None:
                        pairs.append((i * cols + 2 * j + core, a * cols + 2 * b + core))
        return lax.ppermute(value, axes, pairs)

    def along_row(value, steps):
        return move(value, lambda i, core: target_of(i, steps[core], rows), lambda j, core: j)

    def along_depth(value, steps):
        return move(value, lambda i, core: i, lambda j, core: target_of(j, steps[core], depth))

    def both(value, slot):
        def row_of(i, core):
            return i if core == 0 else target_of(i, far_steps(rows)[slot], rows) if slot < rows else None

        def depth_of(j, core):
            return j if core == 1 else target_of(j, far_steps(depth)[slot], depth) if slot < depth else None

        return move(value, row_of, depth_of)

    nodes = lax.broadcasted_iota(jnp.int32, (slab_rows, slab_rows), 0)
    unit = jnp.asarray(np.eye(slab_rows), BF)
    values = jnp.concatenate([grad_out, pre_act, features, unit], axis=1)
    placed = dot((nodes == order[None, :]).astype(BF), values, ((0,), (0,))).astype(BF)
    grad, pre, feat, place = [placed[:, i * F : (i + 1) * F] for i in range(4)]
    masked = jnp.where(pre > 0, grad, jnp.zeros_like(grad))
    message = jnp.concatenate([jnp.where(even, masked, feat), across(jnp.where(even, feat, masked))], axis=0)
    message, counts = lax.optimization_barrier((message, block_counts))
    filled = jnp.arange(K, dtype=jnp.int32)[:, None] < counts[0, 0][None, :]
    targets = jnp.where(filled, block_cols[0, 0].T, 0)
    blocks = jnp.where(filled.T[:, :, None, None], blocks[0, 0], jnp.zeros((), BF))
    steps = max(rows, depth)
    own = [message] + [both(message, slot) for slot in range(1, steps)]
    held, targets, blocks = lax.optimization_barrier((message, targets, blocks))
    other = [across(value) for value in (held, *own[1:])]
    term, weight_term, *messages = call(
        functools.partial(product_kernel, rows, depth),
        [slab, jax.ShapeDtypeStruct((F, F), F32), pair] + [pair] * (rows - 2),
        (targets, blocks, *own, *other),
        [pltpu.VMEM] * (2 + 2 * steps),
        scratch=[
            pltpu.VMEM((rows, B, F), F32),
            pltpu.VMEM((cols * K, B, F), F32),
            pltpu.SMEM(targets.shape, jnp.int32),
            pltpu.SemaphoreType.DMA,
        ],
        limit=limit,
    )
    chip_weight = (weight_term + across(weight_term)).astype(BF)
    plan = row_steps(rows)
    terms = [along_row(messages[0], plan[0])]
    terms += [along_row(m.at[B:].set(chip_weight), plan[i]) for i, m in enumerate(messages) if i > 0]
    (grad_feat,) = call(
        functools.partial(feature_kernel, rows), [slab], (place, weight, term, *terms), [pltpu.VMEM] * (rows + 2)
    )
    mine = terms[1][B:]
    swapped = across(mine)
    weights = [chip_weight, jnp.where(even, swapped, mine), jnp.where(even, mine, swapped)] + [t[B:] for t in terms[2:]]
    row_weight = sum_in_order(weights, r, rows).astype(BF)
    mine = along_depth(row_weight, (1, 2))
    rest = [along_depth(row_weight, (step, step)) for step in range(3, depth)]
    swapped = across(mine)
    weights = [row_weight, jnp.where(even, mine, swapped), jnp.where(even, swapped, mine)] + rest
    summed = sum_in_order(weights, z, depth)
    return grad_feat, summed * (slab_rows * rows * cols) ** (-0.5)


def solution(mesh):
    placed = (
        P(("row", "col"), None),
        P(("row", "col"), None),
        P(("row", "col"), None),
        P(),
        P("row", "col", None, None, None, None),
        P("row", "col", None, None),
        P("row", "col", None),
        P(("row", "col")),
    )
    return jax.shard_map(
        shards,
        mesh=mesh,
        in_specs=placed,
        out_specs=(P(("row", "col"), None), P()),
        check_vma=False,
    )
```

```python
import functools

import jax
import jax.numpy as jnp
import numpy as np
from jax import lax
from jax.experimental import pallas as pl
from jax.experimental.pallas import tpu as pltpu
from jax.sharding import PartitionSpec as P

F = 128
B = 128
K = 2
BF = jnp.bfloat16
F32 = jnp.float32


def swaps(size):
    return size & (size - 1) == 0


def target_of(index, step, size):
    return index ^ step if swaps(size) else (index + step) % size


def source_of(index, step, size):
    return index ^ step if swaps(size) else lax.rem(index + (size - step), size)


def far_steps(size):
    return [0, 1, *range(size - 1, 1, -1)]


def dot(a, b, contract):
    return lax.dot_general(a, b, (contract, ((), ())), preferred_element_type=F32)


def call(body, outs, args, spaces, scratch=(), limit=4 << 20):
    return pl.pallas_call(
        body,
        out_shape=outs,
        in_specs=[pl.BlockSpec(memory_space=space) for space in spaces],
        out_specs=[pl.BlockSpec(memory_space=pltpu.VMEM)] * len(outs),
        scratch_shapes=list(scratch),
        compiler_params=pltpu.CompilerParams(vmem_limit_bytes=limit),
    )(*args)


def row_steps(rows):
    return list(zip([1, 2, *range(3, rows)], [2, 1, *range(3, rows)]))


def product_kernel(rows, depth, *refs):
    steps = max(rows, depth)
    targets_ref, blocks_ref = refs[:2]
    own, other = refs[2 : 2 + steps], refs[2 + steps : 2 + 2 * steps]
    term_ref, weight_ref = refs[2 + 2 * steps : 4 + 2 * steps]
    outs = refs[4 + 2 * steps : -1]
    total = refs[-1]
    r = lax.axis_index("row")
    c = lax.axis_index("col")
    z, even = lax.div(c, 2), lax.rem(c, 2) == 0
    pairs = []
    for slot, step in enumerate(far_steps(depth)):
        pair = jnp.where(even, own[slot][...], other[slot][...])
        pairs.append(pair)
    total[...] = jnp.zeros_like(total)
    targets = targets_ref[...].astype(F32)
    row_at = lax.broadcasted_iota(jnp.int32, targets.shape, 0)
    col_at = lax.broadcasted_iota(jnp.int32, targets.shape, 1)
    for slot, step in enumerate(far_steps(depth)):
        chip = source_of(z, step, depth)
        for core in range(2):
            for k in range(K):
                product = dot(blocks_ref[2 * chip + core, k], pairs[slot][core * B : (core + 1) * B], ((0,), (0,)))
                target = jnp.max(jnp.where((row_at == k) & (col_at == 2 * chip + core), targets, 0.0))
                total[target.astype(jnp.int32)] += product
    terms = [total[source_of(r, step, rows)].astype(BF) for step in range(rows)]
    weight = jnp.zeros((F, F), F32)
    for slot, step in enumerate(far_steps(rows)):
        feat = jnp.where(even, other[slot][B : 2 * B], own[slot][0:B])
        weight += dot(feat, terms[step], ((0,), (0,)))
    term_ref[...] = terms[0]
    weight_ref[...] = weight
    sent = terms if swaps(rows) else [terms[-step] for step in range(rows)]
    for out, (first, second) in zip(outs, row_steps(rows)):
        out[0:B] = jnp.where(even, sent[first], sent[second])
    outs[0][B : 2 * B] = jnp.zeros((B, F), BF)


def sum_in_order(values, index, size):
    values = [v.astype(F32) for v in values]
    if swaps(size):
        while len(values) > 1:
            values = [a + b for a, b in zip(values[0::2], values[1::2])]
        return values[0]
    places = jnp.stack([source_of(index, step, size) for step in range(size)])
    held = jnp.zeros((size,) + values[0].shape, F32).at[places].set(jnp.stack(values))
    return functools.reduce(lambda a, b: a + b, [held[i] for i in range(size)])


def feature_kernel(count, place_ref, weight_ref, *refs):
    terms, out_ref = refs[:count], refs[count]
    total = terms[0][0:B].astype(F32)
    for term in terms[1:]:
        total += term[0:B].astype(F32)
    grad = dot(total.astype(BF), weight_ref[...], ((1,), (1,))).astype(BF)
    out_ref[...] = dot(place_ref[...], grad, ((0,), (0,))).astype(BF)


def shards(grad_out, pre_act, features, weight, blocks, block_cols, block_counts, order):
    slab_rows = grad_out.shape[0]
    rows = lax.axis_size("row")
    cols = lax.axis_size("col")
    depth = cols // 2
    axes = ("row", "col")
    r, c = lax.axis_index("row"), lax.axis_index("col")
    z, even = lax.div(c, 2), lax.rem(c, 2) == 0
    slab = jax.ShapeDtypeStruct((B, F), BF)
    pair = jax.ShapeDtypeStruct((2 * B, F), BF)
    limit = (4 << 20) + 8 * blocks.size

    def across(value):
        return lax.ppermute(value, "col", [(i, i ^ 1) for i in range(cols)])

    def move(value, row_of, depth_of):
        pairs = []
        for i in range(rows):
            for j in range(depth):
                for core in range(2):
                    a, b = row_of(i, core), depth_of(j, core)
                    if a is not None and b is not None:
                        pairs.append((i * cols + 2 * j + core, a * cols + 2 * b + core))
        return lax.ppermute(value, axes, pairs)

    def along_row(value, steps):
        return move(value, lambda i, core: target_of(i, steps[core], rows), lambda j, core: j)

    def along_depth(value, steps):
        return move(value, lambda i, core: i, lambda j, core: target_of(j, steps[core], depth))

    def both(value, slot):
        def row_of(i, core):
            return i if core == 0 else target_of(i, far_steps(rows)[slot], rows) if slot < rows else None

        def depth_of(j, core):
            return j if core == 1 else target_of(j, far_steps(depth)[slot], depth) if slot < depth else None

        return move(value, row_of, depth_of)

    nodes = lax.broadcasted_iota(jnp.int32, (slab_rows, slab_rows), 0)
    unit = jnp.asarray(np.eye(slab_rows), BF)
    values = jnp.concatenate([grad_out, pre_act, features, unit], axis=1)
    placed = dot((nodes == order[None, :]).astype(BF), values, ((0,), (0,))).astype(BF)
    grad, pre, feat, place = [placed[:, i * F : (i + 1) * F] for i in range(4)]
    masked = jnp.where(pre > 0, grad, jnp.zeros_like(grad))
    message = jnp.concatenate([jnp.where(even, masked, feat), across(jnp.where(even, feat, masked))], axis=0)
    message, counts = lax.optimization_barrier((message, block_counts))
    filled = jnp.arange(K, dtype=jnp.int32)[:, None] < counts[0, 0][None, :]
    targets = jnp.where(filled, block_cols[0, 0].T, 0)
    blocks = jnp.where(filled.T[:, :, None, None], blocks[0, 0], jnp.zeros((), BF))
    steps = max(rows, depth)
    own = [message] + [both(message, slot) for slot in range(1, steps)]
    held, targets, blocks = lax.optimization_barrier((message, targets, blocks))
    other = [across(value) for value in (held, *own[1:])]
    term, weight_term, *messages = call(
        functools.partial(product_kernel, rows, depth),
        [slab, jax.ShapeDtypeStruct((F, F), F32), pair] + [pair] * (rows - 2),
        (targets, blocks, *own, *other),
        [pltpu.VMEM] * (2 + 2 * steps),
        scratch=[
            pltpu.VMEM((rows, B, F), F32),
        ],
        limit=limit,
    )
    chip_weight = (weight_term + across(weight_term)).astype(BF)
    plan = row_steps(rows)
    terms = [along_row(messages[0], plan[0])]
    terms += [along_row(m.at[B:].set(chip_weight), plan[i]) for i, m in enumerate(messages) if i > 0]
    (grad_feat,) = call(
        functools.partial(feature_kernel, rows), [slab], (place, weight, term, *terms), [pltpu.VMEM] * (rows + 2)
    )
    mine = terms[1][B:]
    swapped = across(mine)
    weights = [chip_weight, jnp.where(even, swapped, mine), jnp.where(even, mine, swapped)] + [t[B:] for t in terms[2:]]
    row_weight = sum_in_order(weights, r, rows).astype(BF)
    mine = along_depth(row_weight, (1, 2))
    rest = [along_depth(row_weight, (step, step)) for step in range(3, depth)]
    swapped = across(mine)
    weights = [row_weight, jnp.where(even, mine, swapped), jnp.where(even, swapped, mine)] + rest
    summed = sum_in_order(weights, z, depth)
    return grad_feat, summed * (slab_rows * rows * cols) ** (-0.5)


def solution(mesh):
    placed = (
        P(("row", "col"), None),
        P(("row", "col"), None),
        P(("row", "col"), None),
        P(),
        P("row", "col", None, None, None, None),
        P("row", "col", None, None),
        P("row", "col", None),
        P(("row", "col")),
    )
    return jax.shard_map(
        shards,
        mesh=mesh,
        in_specs=placed,
        out_specs=(P(("row", "col"), None), P()),
        check_vma=False,
    )
```

```python
import functools

import jax
import jax.numpy as jnp
import numpy as np
from jax import lax
from jax.experimental import pallas as pl
from jax.experimental.pallas import tpu as pltpu
from jax.sharding import PartitionSpec as P

F = 128
B = 128
K = 2
BF = jnp.bfloat16
F32 = jnp.float32


def swaps(size):
    return size & (size - 1) == 0


def target_of(index, step, size):
    return index ^ step if swaps(size) else (index + step) % size


def source_of(index, step, size):
    return index ^ step if swaps(size) else lax.rem(index + (size - step), size)


def far_steps(size):
    return [0, 1, *range(size - 1, 1, -1)]


def dot(a, b, contract):
    return lax.dot_general(a, b, (contract, ((), ())), preferred_element_type=F32)


def call(body, outs, args, spaces, scratch=(), limit=4 << 20):
    return pl.pallas_call(
        body,
        out_shape=outs,
        in_specs=[pl.BlockSpec(memory_space=space) for space in spaces],
        out_specs=[pl.BlockSpec(memory_space=pltpu.VMEM)] * len(outs),
        scratch_shapes=list(scratch),
        compiler_params=pltpu.CompilerParams(vmem_limit_bytes=limit),
    )(*args)


def row_steps(rows):
    return list(zip([2, 1, *range(3, rows)], [1, 2, *range(3, rows)]))


def product_kernel(rows, depth, *refs):
    steps = max(rows, depth)
    targets_ref, blocks_ref = refs[:2]
    own, other = refs[2 : 2 + steps], refs[2 + steps : 2 + 2 * steps]
    term_ref, weight_ref = refs[2 + 2 * steps : 4 + 2 * steps]
    outs = refs[4 + 2 * steps : -1]
    total = refs[-1]
    r = lax.axis_index("row")
    c = lax.axis_index("col")
    z, even = lax.div(c, 2), lax.rem(c, 2) == 0
    pairs = []
    for slot, step in enumerate(far_steps(depth)):
        pair = jnp.where(even, own[slot][...], other[slot][...])
        pairs.append(pair)
    total[...] = jnp.zeros_like(total)
    targets = targets_ref[...].astype(F32)
    row_at = lax.broadcasted_iota(jnp.int32, targets.shape, 0)
    col_at = lax.broadcasted_iota(jnp.int32, targets.shape, 1)
    for slot, step in enumerate(far_steps(depth)):
        chip = source_of(z, step, depth)
        for core in range(2):
            for k in range(K):
                product = dot(blocks_ref[2 * chip + core, k], pairs[slot][core * B : (core + 1) * B], ((0,), (0,)))
                target = jnp.max(jnp.where((row_at == k) & (col_at == 2 * chip + core), targets, 0.0))
                total[target.astype(jnp.int32)] += product
    terms = [total[source_of(r, step, rows)].astype(BF) for step in range(rows)]
    weight = jnp.zeros((F, F), F32)
    for slot, step in enumerate(far_steps(rows)):
        feat = jnp.where(even, other[slot][B : 2 * B], own[slot][0:B])
        weight += dot(feat, terms[step], ((0,), (0,)))
    term_ref[...] = terms[0]
    weight_ref[...] = weight
    sent = terms if swaps(rows) else [terms[-step] for step in range(rows)]
    for out, (first, second) in zip(outs, row_steps(rows)):
        out[0:B] = jnp.where(even, sent[first], sent[second])
    outs[0][B : 2 * B] = jnp.zeros((B, F), BF)


def sum_in_order(values, index, size):
    values = [v.astype(F32) for v in values]
    if swaps(size):
        while len(values) > 1:
            values = [a + b for a, b in zip(values[0::2], values[1::2])]
        return values[0]
    places = jnp.stack([source_of(index, step, size) for step in range(size)])
    held = jnp.zeros((size,) + values[0].shape, F32).at[places].set(jnp.stack(values))
    return functools.reduce(lambda a, b: a + b, [held[i] for i in range(size)])


def feature_kernel(count, place_ref, weight_ref, *refs):
    terms, out_ref = refs[:count], refs[count]
    total = terms[0][0:B].astype(F32)
    for term in terms[1:]:
        total += term[0:B].astype(F32)
    grad = dot(total.astype(BF), weight_ref[...], ((1,), (1,))).astype(BF)
    out_ref[...] = dot(place_ref[...], grad, ((0,), (0,))).astype(BF)


def shards(grad_out, pre_act, features, weight, blocks, block_cols, block_counts, order):
    slab_rows = grad_out.shape[0]
    rows = lax.axis_size("row")
    cols = lax.axis_size("col")
    depth = cols // 2
    axes = ("row", "col")
    r, c = lax.axis_index("row"), lax.axis_index("col")
    z, even = lax.div(c, 2), lax.rem(c, 2) == 0
    slab = jax.ShapeDtypeStruct((B, F), BF)
    pair = jax.ShapeDtypeStruct((2 * B, F), BF)
    limit = (4 << 20) + 8 * blocks.size

    def across(value):
        return lax.ppermute(value, "col", [(i, i ^ 1) for i in range(cols)])

    def move(value, row_of, depth_of):
        pairs = []
        for i in range(rows):
            for j in range(depth):
                for core in range(2):
                    a, b = row_of(i, core), depth_of(j, core)
                    if a is not None and b is not None:
                        pairs.append((i * cols + 2 * j + core, a * cols + 2 * b + core))
        return lax.ppermute(value, axes, pairs)

    def along_row(value, steps):
        return move(value, lambda i, core: target_of(i, steps[core], rows), lambda j, core: j)

    def along_depth(value, steps):
        return move(value, lambda i, core: i, lambda j, core: target_of(j, steps[core], depth))

    def both(value, slot):
        def row_of(i, core):
            return i if core == 0 else target_of(i, far_steps(rows)[slot], rows) if slot < rows else None

        def depth_of(j, core):
            return j if core == 1 else target_of(j, far_steps(depth)[slot], depth) if slot < depth else None

        return move(value, row_of, depth_of)

    nodes = lax.broadcasted_iota(jnp.int32, (slab_rows, slab_rows), 0)
    unit = jnp.asarray(np.eye(slab_rows), BF)
    values = jnp.concatenate([grad_out, pre_act, features, unit], axis=1)
    placed = dot((nodes == order[None, :]).astype(BF), values, ((0,), (0,))).astype(BF)
    grad, pre, feat, place = [placed[:, i * F : (i + 1) * F] for i in range(4)]
    masked = jnp.where(pre > 0, grad, jnp.zeros_like(grad))
    message = jnp.concatenate([jnp.where(even, masked, feat), across(jnp.where(even, feat, masked))], axis=0)
    message, counts = lax.optimization_barrier((message, block_counts))
    filled = jnp.arange(K, dtype=jnp.int32)[:, None] < counts[0, 0][None, :]
    targets = jnp.where(filled, block_cols[0, 0].T, 0)
    blocks = jnp.where(filled.T[:, :, None, None], blocks[0, 0], jnp.zeros((), BF))
    steps = max(rows, depth)
    own = [message] + [both(message, slot) for slot in range(1, steps)]
    held, targets, blocks = lax.optimization_barrier((message, targets, blocks))
    other = [across(value) for value in (held, *own[1:])]
    term, weight_term, *messages = call(
        functools.partial(product_kernel, rows, depth),
        [slab, jax.ShapeDtypeStruct((F, F), F32), pair] + [pair] * (rows - 2),
        (targets, blocks, *own, *other),
        [pltpu.VMEM] * (2 + 2 * steps),
        scratch=[
            pltpu.VMEM((rows, B, F), F32),
        ],
        limit=limit,
    )
    chip_weight = (weight_term + across(weight_term)).astype(BF)
    plan = row_steps(rows)
    terms = [along_row(messages[0], plan[0])]
    terms += [along_row(m.at[B:].set(chip_weight), plan[i]) for i, m in enumerate(messages) if i > 0]
    (grad_feat,) = call(
        functools.partial(feature_kernel, rows), [slab], (place, weight, term, *terms), [pltpu.VMEM] * (rows + 2)
    )
    mine = terms[1][B:]
    swapped = across(mine)
    weights = {0: chip_weight, 1: jnp.where(even, mine, swapped), 2: jnp.where(even, swapped, mine)}
    weights.update({plan[k][0]: term[B:] for k, term in enumerate(terms) if k > 1})
    row_weight = sum_in_order([weights[step] for step in range(rows)], r, rows).astype(BF)
    last = depth - 1
    mine = along_depth(row_weight, (1, last))
    weights = {step: along_depth(row_weight, (step, step)) for step in range(2, last)}
    swapped = across(mine)
    weights.update({0: row_weight, 1: jnp.where(even, mine, swapped), last: jnp.where(even, swapped, mine)})
    summed = sum_in_order([weights[step] for step in range(depth)], z, depth)
    return grad_feat, summed * (slab_rows * rows * cols) ** (-0.5)


def solution(mesh):
    placed = (
        P(("row", "col"), None),
        P(("row", "col"), None),
        P(("row", "col"), None),
        P(),
        P("row", "col", None, None, None, None),
        P("row", "col", None, None),
        P("row", "col", None),
        P(("row", "col")),
    )
    return jax.shard_map(
        shards,
        mesh=mesh,
        in_specs=placed,
        out_specs=(P(("row", "col"), None), P()),
        check_vma=False,
    )
```

```python
import functools

import jax
import jax.numpy as jnp
import numpy as np
from jax import lax
from jax.experimental import pallas as pl
from jax.experimental.pallas import tpu as pltpu
from jax.sharding import PartitionSpec as P

F = 128
B = 128
K = 2
BF = jnp.bfloat16
F32 = jnp.float32


def swaps(size):
    return size & (size - 1) == 0


def target_of(index, step, size):
    return index ^ step if swaps(size) else (index + step) % size


def source_of(index, step, size):
    return index ^ step if swaps(size) else lax.rem(index + (size - step), size)


def far_steps(size):
    return [0, 1, *range(size - 1, 1, -1)]


def row_slots(rows):
    return [0, 2, 1, *range(3, rows)]


def dot(a, b, contract):
    return lax.dot_general(a, b, (contract, ((), ())), preferred_element_type=F32)


def call(body, outs, args, spaces, scratch=(), limit=4 << 20):
    return pl.pallas_call(
        body,
        out_shape=outs,
        in_specs=[pl.BlockSpec(memory_space=space) for space in spaces],
        out_specs=[pl.BlockSpec(memory_space=pltpu.VMEM)] * len(outs),
        scratch_shapes=list(scratch),
        compiler_params=pltpu.CompilerParams(vmem_limit_bytes=limit),
    )(*args)


def row_steps(rows):
    return list(zip([1, 2, *range(3, rows)], [2, 1, *range(3, rows)]))


def product_kernel(rows, depth, *refs):
    steps = max(rows, depth)
    targets_ref, blocks_ref = refs[:2]
    own, other = refs[2 : 2 + steps], refs[2 + steps : 2 + 2 * steps]
    term_ref, weight_ref = refs[2 + 2 * steps : 4 + 2 * steps]
    outs = refs[4 + 2 * steps : -1]
    total = refs[-1]
    r = lax.axis_index("row")
    c = lax.axis_index("col")
    z, even = lax.div(c, 2), lax.rem(c, 2) == 0
    pairs = []
    for slot, step in enumerate(far_steps(depth)):
        pair = jnp.where(even, other[slot][...], own[slot][...])
        pairs.append(pair)
    total[...] = jnp.zeros_like(total)
    targets = targets_ref[...].astype(F32)
    row_at = lax.broadcasted_iota(jnp.int32, targets.shape, 0)
    col_at = lax.broadcasted_iota(jnp.int32, targets.shape, 1)
    for slot, step in enumerate(far_steps(depth)):
        chip = source_of(z, step, depth)
        for part in range(2):
            i = 2 * chip + 1 - part
            for k in range(K):
                product = dot(blocks_ref[i, k], pairs[slot][part * B : (part + 1) * B], ((0,), (0,)))
                target = jnp.max(jnp.where((row_at == k) & (col_at == i), targets, 0.0))
                total[target.astype(jnp.int32)] += product
    terms = [total[source_of(r, step, rows)].astype(BF) for step in range(rows)]
    weight = jnp.zeros((F, F), F32)
    for slot, step in enumerate(row_slots(rows)):
        feat = jnp.where(even, own[slot][0:B], other[slot][B : 2 * B])
        weight += dot(feat, terms[step], ((0,), (0,)))
    term_ref[...] = terms[0]
    weight_ref[...] = weight
    sent = terms if swaps(rows) else [terms[-step] for step in range(rows)]
    for out, (first, second) in zip(outs, row_steps(rows)):
        out[0:B] = jnp.where(even, sent[first], sent[second])
    outs[0][B : 2 * B] = jnp.zeros((B, F), BF)


def sum_in_order(values, index, size):
    values = [v.astype(F32) for v in values]
    if swaps(size):
        while len(values) > 1:
            values = [a + b for a, b in zip(values[0::2], values[1::2])]
        return values[0]
    places = jnp.stack([source_of(index, step, size) for step in range(size)])
    held = jnp.zeros((size,) + values[0].shape, F32).at[places].set(jnp.stack(values))
    return functools.reduce(lambda a, b: a + b, [held[i] for i in range(size)])


def feature_kernel(count, place_ref, weight_ref, *refs):
    terms, out_ref = refs[:count], refs[count]
    total = terms[0][0:B].astype(F32)
    for term in terms[1:]:
        total += term[0:B].astype(F32)
    grad = dot(total.astype(BF), weight_ref[...], ((1,), (1,))).astype(BF)
    out_ref[...] = dot(place_ref[...], grad, ((0,), (0,))).astype(BF)


def shards(grad_out, pre_act, features, weight, blocks, block_cols, block_counts, order):
    slab_rows = grad_out.shape[0]
    rows = lax.axis_size("row")
    cols = lax.axis_size("col")
    depth = cols // 2
    axes = ("row", "col")
    r, c = lax.axis_index("row"), lax.axis_index("col")
    z, even = lax.div(c, 2), lax.rem(c, 2) == 0
    slab = jax.ShapeDtypeStruct((B, F), BF)
    pair = jax.ShapeDtypeStruct((2 * B, F), BF)
    limit = (4 << 20) + 8 * blocks.size

    def across(value):
        return lax.ppermute(value, "col", [(i, i ^ 1) for i in range(cols)])

    def move(value, row_of, depth_of):
        pairs = []
        for i in range(rows):
            for j in range(depth):
                for core in range(2):
                    a, b = row_of(i, core), depth_of(j, core)
                    if a is not None and b is not None:
                        pairs.append((i * cols + 2 * j + core, a * cols + 2 * b + core))
        return lax.ppermute(value, axes, pairs)

    def along_row(value, steps):
        return move(value, lambda i, core: target_of(i, steps[core], rows), lambda j, core: j)

    def along_depth(value, steps):
        return move(value, lambda i, core: i, lambda j, core: target_of(j, steps[core], depth))

    def both(value, slot):
        def row_of(i, core):
            if core == 1:
                return i
            return target_of(i, row_slots(rows)[slot], rows) if slot < rows else None

        def depth_of(j, core):
            if core == 0:
                return j
            return target_of(j, far_steps(depth)[slot], depth) if slot < depth else None

        return move(value, row_of, depth_of)

    nodes = lax.broadcasted_iota(jnp.int32, (slab_rows, slab_rows), 0)
    unit = jnp.asarray(np.eye(slab_rows), BF)
    values = jnp.concatenate([grad_out, pre_act, features, unit], axis=1)
    placed = dot((nodes == order[None, :]).astype(BF), values, ((0,), (0,))).astype(BF)
    grad, pre, feat, place = [placed[:, i * F : (i + 1) * F] for i in range(4)]
    masked = jnp.where(pre > 0, grad, jnp.zeros_like(grad))
    message = jnp.concatenate([jnp.where(even, feat, masked), across(jnp.where(even, masked, feat))], axis=0)
    message, counts = lax.optimization_barrier((message, block_counts))
    filled = jnp.arange(K, dtype=jnp.int32)[:, None] < counts[0, 0][None, :]
    targets = jnp.where(filled, block_cols[0, 0].T, 0)
    blocks = jnp.where(filled.T[:, :, None, None], blocks[0, 0], jnp.zeros((), BF))
    steps = max(rows, depth)
    own = [message] + [both(message, slot) for slot in range(1, steps)]
    held, targets, blocks = lax.optimization_barrier((message, targets, blocks))
    other = [across(value) for value in (held, *own[1:])]
    term, weight_term, *messages = call(
        functools.partial(product_kernel, rows, depth),
        [slab, jax.ShapeDtypeStruct((F, F), F32), pair] + [pair] * (rows - 2),
        (targets, blocks, *own, *other),
        [pltpu.VMEM] * (2 + 2 * steps),
        scratch=[
            pltpu.VMEM((rows, B, F), F32),
        ],
        limit=limit,
    )
    chip_weight = (weight_term + across(weight_term)).astype(BF)
    plan = row_steps(rows)
    terms = [along_row(messages[0], plan[0])]
    terms += [along_row(m.at[B:].set(chip_weight), plan[i]) for i, m in enumerate(messages) if i > 0]
    (grad_feat,) = call(
        functools.partial(feature_kernel, rows), [slab], (place, weight, term, *terms), [pltpu.VMEM] * (rows + 2)
    )
    mine = terms[1][B:]
    swapped = across(mine)
    weights = {0: chip_weight, 2: jnp.where(even, mine, swapped), 1: jnp.where(even, swapped, mine)}
    weights.update({plan[k][0]: term[B:] for k, term in enumerate(terms) if k > 1})
    row_weight = sum_in_order([weights[step] for step in range(rows)], r, rows).astype(BF)
    first, second = depth - 2, depth - 1
    mine = along_depth(row_weight, (first, second))
    weights = {step: along_depth(row_weight, (step, step)) for step in range(1, first)}
    swapped = across(mine)
    weights.update({0: row_weight, first: jnp.where(even, mine, swapped), second: jnp.where(even, swapped, mine)})
    summed = sum_in_order([weights[step] for step in range(depth)], z, depth)
    return grad_feat, summed * (slab_rows * rows * cols) ** (-0.5)


def solution(mesh):
    placed = (
        P(("row", "col"), None),
        P(("row", "col"), None),
        P(("row", "col"), None),
        P(),
        P("row", "col", None, None, None, None),
        P("row", "col", None, None),
        P("row", "col", None),
        P(("row", "col")),
    )
    return jax.shard_map(
        shards,
        mesh=mesh,
        in_specs=placed,
        out_specs=(P(("row", "col"), None), P()),
        check_vma=False,
    )
```

```python
import functools

import jax
import jax.numpy as jnp
import numpy as np
from jax import lax
from jax.experimental import pallas as pl
from jax.experimental.pallas import tpu as pltpu
from jax.sharding import PartitionSpec as P

F = 128
B = 128
K = 2
BF = jnp.bfloat16
F32 = jnp.float32


def swaps(size):
    return size & (size - 1) == 0


def target_of(index, step, size):
    return index ^ step if swaps(size) else (index + step) % size


def source_of(index, step, size):
    return index ^ step if swaps(size) else lax.rem(index + (size - step), size)


def far_steps(size):
    return [0, 1, *range(size - 1, 1, -1)]


def row_slots(rows):
    return [0, *range(2, rows), 1]


def dot(a, b, contract):
    return lax.dot_general(a, b, (contract, ((), ())), preferred_element_type=F32)


def call(body, outs, args, spaces, scratch=(), limit=4 << 20):
    return pl.pallas_call(
        body,
        out_shape=outs,
        in_specs=[pl.BlockSpec(memory_space=space) for space in spaces],
        out_specs=[pl.BlockSpec(memory_space=pltpu.VMEM)] * len(outs),
        scratch_shapes=list(scratch),
        compiler_params=pltpu.CompilerParams(vmem_limit_bytes=limit),
    )(*args)


def row_steps(rows):
    return list(zip([1, 2, *range(3, rows)], [2, 1, *range(3, rows)]))


def product_kernel(rows, depth, *refs):
    steps = max(rows, depth)
    targets_ref, blocks_ref = refs[:2]
    own, other = refs[2 : 2 + steps], refs[2 + steps : 2 + 2 * steps]
    term_ref, weight_ref = refs[2 + 2 * steps : 4 + 2 * steps]
    outs = refs[4 + 2 * steps : -1]
    total = refs[-1]
    r = lax.axis_index("row")
    c = lax.axis_index("col")
    z, even = lax.div(c, 2), lax.rem(c, 2) == 0
    pairs = []
    for slot, step in enumerate(far_steps(depth)):
        pair = jnp.where(even, other[slot][...], own[slot][...])
        pairs.append(pair)
    total[...] = jnp.zeros_like(total)
    targets = targets_ref[...].astype(F32)
    row_at = lax.broadcasted_iota(jnp.int32, targets.shape, 0)
    col_at = lax.broadcasted_iota(jnp.int32, targets.shape, 1)
    for slot, step in enumerate(far_steps(depth)):
        chip = source_of(z, step, depth)
        for part in range(2):
            i = 2 * chip + 1 - part
            for k in range(K):
                product = dot(blocks_ref[i, k], pairs[slot][part * B : (part + 1) * B], ((0,), (0,)))
                target = jnp.max(jnp.where((row_at == k) & (col_at == i), targets, 0.0))
                total[target.astype(jnp.int32)] += product
    terms = [total[source_of(r, step, rows)].astype(BF) for step in range(rows)]
    weight = jnp.zeros((F, F), F32)
    for slot, step in enumerate(row_slots(rows)):
        feat = jnp.where(even, own[slot][0:B], other[slot][B : 2 * B])
        weight += dot(feat, terms[step], ((0,), (0,)))
    term_ref[...] = terms[0]
    weight_ref[...] = weight
    sent = terms if swaps(rows) else [terms[-step] for step in range(rows)]
    for out, (first, second) in zip(outs, row_steps(rows)):
        out[0:B] = jnp.where(even, sent[first], sent[second])
    outs[0][B : 2 * B] = jnp.zeros((B, F), BF)


def sum_in_order(values, index, size):
    values = [v.astype(F32) for v in values]
    if swaps(size):
        while len(values) > 1:
            values = [a + b for a, b in zip(values[0::2], values[1::2])]
        return values[0]
    places = jnp.stack([source_of(index, step, size) for step in range(size)])
    held = jnp.zeros((size,) + values[0].shape, F32).at[places].set(jnp.stack(values))
    return functools.reduce(lambda a, b: a + b, [held[i] for i in range(size)])


def feature_kernel(count, place_ref, weight_ref, *refs):
    terms, out_ref = refs[:count], refs[count]
    total = terms[0][0:B].astype(F32)
    for term in terms[1:]:
        total += term[0:B].astype(F32)
    grad = dot(total.astype(BF), weight_ref[...], ((1,), (1,))).astype(BF)
    out_ref[...] = dot(place_ref[...], grad, ((0,), (0,))).astype(BF)


def last_kernel(scale, grad_ref, weight_ref, grad_out, weight_out):
    grad_out[...] = grad_ref[...]
    weight_out[...] = weight_ref[...] * scale


def shards(grad_out, pre_act, features, weight, blocks, block_cols, block_counts, order):
    slab_rows = grad_out.shape[0]
    rows = lax.axis_size("row")
    cols = lax.axis_size("col")
    depth = cols // 2
    axes = ("row", "col")
    r, c = lax.axis_index("row"), lax.axis_index("col")
    z, even = lax.div(c, 2), lax.rem(c, 2) == 0
    slab = jax.ShapeDtypeStruct((B, F), BF)
    pair = jax.ShapeDtypeStruct((2 * B, F), BF)
    limit = (4 << 20) + 8 * blocks.size

    def across(value):
        return lax.ppermute(value, "col", [(i, i ^ 1) for i in range(cols)])

    def move(value, row_of, depth_of):
        pairs = []
        for i in range(rows):
            for j in range(depth):
                for core in range(2):
                    a, b = row_of(i, core), depth_of(j, core)
                    if a is not None and b is not None:
                        pairs.append((i * cols + 2 * j + core, a * cols + 2 * b + core))
        return lax.ppermute(value, axes, pairs)

    def along_row(value, steps):
        return move(value, lambda i, core: target_of(i, steps[core], rows), lambda j, core: j)

    def along_depth(value, steps):
        return move(value, lambda i, core: i, lambda j, core: target_of(j, steps[core], depth))

    def both(value, slot):
        def row_of(i, core):
            if core == 1:
                return i
            return target_of(i, row_slots(rows)[slot], rows) if slot < rows else None

        def depth_of(j, core):
            if core == 0:
                return j
            return target_of(j, far_steps(depth)[slot], depth) if slot < depth else None

        return move(value, row_of, depth_of)

    nodes = lax.broadcasted_iota(jnp.int32, (slab_rows, slab_rows), 0)
    unit = jnp.asarray(np.eye(slab_rows), BF)
    values = jnp.concatenate([grad_out, pre_act, features, unit], axis=1)
    placed = dot((nodes == order[None, :]).astype(BF), values, ((0,), (0,))).astype(BF)
    grad, pre, feat, place = [placed[:, i * F : (i + 1) * F] for i in range(4)]
    masked = jnp.where(pre > 0, grad, jnp.zeros_like(grad))
    message = jnp.concatenate([jnp.where(even, feat, masked), across(jnp.where(even, masked, feat))], axis=0)
    message, counts = lax.optimization_barrier((message, block_counts))
    filled = jnp.arange(K, dtype=jnp.int32)[:, None] < counts[0, 0][None, :]
    used = jnp.arange(K, dtype=jnp.int32)[:, None] < block_counts[0, 0][None, :]
    targets = jnp.where(used, block_cols[0, 0].T, 0)
    blocks = jnp.where(filled.T[:, :, None, None], blocks[0, 0], jnp.zeros((), BF))
    steps = max(rows, depth)
    own = [message] + [both(message, slot) for slot in range(1, steps)]
    held, blocks = lax.optimization_barrier((message, blocks))
    other = [across(value) for value in (held, *own[1:])]
    term, weight_term, *messages = call(
        functools.partial(product_kernel, rows, depth),
        [slab, jax.ShapeDtypeStruct((F, F), F32), pair] + [pair] * (rows - 2),
        (targets, blocks, *own, *other),
        [pltpu.VMEM] * (2 + 2 * steps),
        scratch=[
            pltpu.VMEM((rows, B, F), F32),
        ],
        limit=limit,
    )
    chip_weight = (weight_term + across(weight_term)).astype(BF)
    plan = row_steps(rows)
    terms = [along_row(messages[0], plan[0])]
    terms += [along_row(m.at[B:].set(chip_weight), plan[i]) for i, m in enumerate(messages) if i > 0]
    (grad_feat,) = call(
        functools.partial(feature_kernel, rows), [slab], (place, weight, term, *terms), [pltpu.VMEM] * (rows + 2)
    )
    mine = terms[1][B:]
    swapped = across(mine)
    weights = {0: chip_weight, 2: jnp.where(even, mine, swapped), 1: jnp.where(even, swapped, mine)}
    weights.update({plan[k][0]: term[B:] for k, term in enumerate(terms) if k > 1})
    row_weight = sum_in_order([weights[step] for step in range(rows)], r, rows).astype(BF)
    first, second = depth - 2, depth - 1
    mine = along_depth(row_weight, (first, second))
    weights = {step: along_depth(row_weight, (step, step)) for step in range(1, first)}
    swapped = across(mine)
    weights.update({0: row_weight, first: jnp.where(even, mine, swapped), second: jnp.where(even, swapped, mine)})
    scale = (slab_rows * rows * cols) ** (-0.5)
    summed = sum_in_order([weights[step] for step in range(depth)], z, depth)
    grad_feat, summed = call(
        functools.partial(last_kernel, scale), [slab, jax.ShapeDtypeStruct((F, F), F32)], (grad_feat, summed), [pltpu.VMEM] * 2
    )
    return grad_feat, summed


def solution(mesh):
    placed = (
        P(("row", "col"), None),
        P(("row", "col"), None),
        P(("row", "col"), None),
        P(),
        P("row", "col", None, None, None, None),
        P("row", "col", None, None),
        P("row", "col", None),
        P(("row", "col")),
    )
    return jax.shard_map(
        shards,
        mesh=mesh,
        in_specs=placed,
        out_specs=(P(("row", "col"), None), P()),
        check_vma=False,
    )
```

```python
import functools

import jax
import jax.numpy as jnp
import numpy as np
from jax import lax
from jax.experimental import pallas as pl
from jax.experimental.pallas import tpu as pltpu
from jax.sharding import PartitionSpec as P

F = 128
B = 128
K = 2
BF = jnp.bfloat16
F32 = jnp.float32


def swaps(size):
    return size & (size - 1) == 0


def target_of(index, step, size):
    return index ^ step if swaps(size) else (index + step) % size


def source_of(index, step, size):
    return index ^ step if swaps(size) else lax.rem(index + (size - step), size)


def far_steps(size):
    return [0, 1, *range(size - 1, 1, -1)]


def row_slots(rows):
    return [0, *range(2, rows), 1]


def dot(a, b, contract):
    return lax.dot_general(a, b, (contract, ((), ())), preferred_element_type=F32)


def call(body, outs, args, spaces, scratch=(), limit=4 << 20):
    return pl.pallas_call(
        body,
        out_shape=outs,
        in_specs=[pl.BlockSpec(memory_space=space) for space in spaces],
        out_specs=[pl.BlockSpec(memory_space=pltpu.VMEM)] * len(outs),
        scratch_shapes=list(scratch),
        compiler_params=pltpu.CompilerParams(vmem_limit_bytes=limit),
    )(*args)


def row_steps(rows):
    return list(zip([1, 2, *range(3, rows)], [2, 1, *range(3, rows)]))


def product_kernel(rows, depth, *refs):
    steps = max(rows, depth)
    targets_ref, blocks_ref = refs[:2]
    own, other = refs[2 : 2 + steps], refs[2 + steps : 2 + 2 * steps]
    term_ref, weight_ref = refs[2 + 2 * steps : 4 + 2 * steps]
    outs = refs[4 + 2 * steps : -1]
    total = refs[-1]
    r = lax.axis_index("row")
    c = lax.axis_index("col")
    z, even = lax.div(c, 2), lax.rem(c, 2) == 0
    pairs = []
    for slot, step in enumerate(far_steps(depth)):
        pair = jnp.where(even, other[slot][...], own[slot][...])
        pairs.append(pair)
    total[...] = jnp.zeros_like(total)
    targets = targets_ref[...].astype(F32)
    row_at = lax.broadcasted_iota(jnp.int32, targets.shape, 0)
    col_at = lax.broadcasted_iota(jnp.int32, targets.shape, 1)
    for slot, step in enumerate(far_steps(depth)):
        chip = source_of(z, step, depth)
        for part in range(2):
            i = 2 * chip + 1 - part
            for k in range(K):
                product = dot(blocks_ref[i, k], pairs[slot][part * B : (part + 1) * B], ((0,), (0,)))
                target = jnp.max(jnp.where((row_at == k) & (col_at == i), targets, 0.0))
                total[target.astype(jnp.int32)] += product
    terms = [total[source_of(r, step, rows)].astype(BF) for step in range(rows)]
    weight = jnp.zeros((F, F), F32)
    for slot, step in enumerate(row_slots(rows)):
        feat = jnp.where(even, own[slot][0:B], other[slot][B : 2 * B])
        weight += dot(feat, terms[step], ((0,), (0,)))
    term_ref[...] = terms[0]
    weight_ref[...] = weight.astype(BF)
    sent = terms if swaps(rows) else [terms[-step] for step in range(rows)]
    for out, (first, second) in zip(outs, row_steps(rows)):
        out[0:B] = jnp.where(even, sent[first], sent[second])
    outs[0][B : 2 * B] = jnp.zeros((B, F), BF)


def sum_in_order(values, index, size):
    values = [v.astype(F32) for v in values]
    if swaps(size):
        while len(values) > 1:
            values = [a + b for a, b in zip(values[0::2], values[1::2])]
        return values[0]
    places = jnp.stack([source_of(index, step, size) for step in range(size)])
    held = jnp.zeros((size,) + values[0].shape, F32).at[places].set(jnp.stack(values))
    return functools.reduce(lambda a, b: a + b, [held[i] for i in range(size)])


def feature_kernel(count, place_ref, weight_ref, *refs):
    terms, out_ref = refs[:count], refs[count]
    total = terms[0][0:B].astype(F32)
    for term in terms[1:]:
        total += term[0:B].astype(F32)
    grad = dot(total.astype(BF), weight_ref[...], ((1,), (1,))).astype(BF)
    out_ref[...] = dot(place_ref[...], grad, ((0,), (0,))).astype(BF)


def last_kernel(scale, grad_ref, weight_ref, grad_out, weight_out):
    grad_out[...] = grad_ref[...]
    weight_out[...] = weight_ref[...] * scale


def shards(grad_out, pre_act, features, weight, blocks, block_cols, block_counts, order):
    slab_rows = grad_out.shape[0]
    rows = lax.axis_size("row")
    cols = lax.axis_size("col")
    depth = cols // 2
    axes = ("row", "col")
    r, c = lax.axis_index("row"), lax.axis_index("col")
    z, even = lax.div(c, 2), lax.rem(c, 2) == 0
    slab = jax.ShapeDtypeStruct((B, F), BF)
    pair = jax.ShapeDtypeStruct((2 * B, F), BF)
    limit = (4 << 20) + 8 * blocks.size

    def across(value):
        return lax.ppermute(value, "col", [(i, i ^ 1) for i in range(cols)])

    def move(value, row_of, depth_of):
        pairs = []
        for i in range(rows):
            for j in range(depth):
                for core in range(2):
                    a, b = row_of(i, core), depth_of(j, core)
                    if a is not None and b is not None:
                        pairs.append((i * cols + 2 * j + core, a * cols + 2 * b + core))
        return lax.ppermute(value, axes, pairs)

    def along_row(value, steps):
        return move(value, lambda i, core: target_of(i, steps[core], rows), lambda j, core: j)

    def along_depth(value, steps):
        return move(value, lambda i, core: i, lambda j, core: target_of(j, steps[core], depth))

    def both(value, slot):
        def row_of(i, core):
            if core == 1:
                return i
            return target_of(i, row_slots(rows)[slot], rows) if slot < rows else None

        def depth_of(j, core):
            if core == 0:
                return j
            return target_of(j, far_steps(depth)[slot], depth) if slot < depth else None

        return move(value, row_of, depth_of)

    nodes = lax.broadcasted_iota(jnp.int32, (slab_rows, slab_rows), 0)
    unit = jnp.asarray(np.eye(slab_rows), BF)
    values = jnp.concatenate([grad_out, pre_act, features, unit], axis=1)
    placed = dot((nodes == order[None, :]).astype(BF), values, ((0,), (0,))).astype(BF)
    grad, pre, feat, place = [placed[:, i * F : (i + 1) * F] for i in range(4)]
    masked = jnp.where(pre > 0, grad, jnp.zeros_like(grad))
    message = jnp.concatenate([jnp.where(even, feat, masked), across(jnp.where(even, masked, feat))], axis=0)
    message, counts = lax.optimization_barrier((message, block_counts))
    filled = jnp.arange(K, dtype=jnp.int32)[:, None] < counts[0, 0][None, :]
    used = jnp.arange(K, dtype=jnp.int32)[:, None] < block_counts[0, 0][None, :]
    targets = jnp.where(used, block_cols[0, 0].T, 0)
    blocks = jnp.where(filled.T[:, :, None, None], blocks[0, 0], jnp.zeros((), BF))
    steps = max(rows, depth)
    own = [message] + [both(message, slot) for slot in range(1, steps)]
    held, blocks = lax.optimization_barrier((message, blocks))
    other = [across(value) for value in (held, *own[1:])]
    term, weight_term, *messages = call(
        functools.partial(product_kernel, rows, depth),
        [slab, slab, pair] + [pair] * (rows - 2),
        (targets, blocks, *own, *other),
        [pltpu.VMEM] * (2 + 2 * steps),
        scratch=[
            pltpu.VMEM((rows, B, F), F32),
        ],
        limit=limit,
    )
    chip_weight = (weight_term.astype(F32) + across(weight_term).astype(F32)).astype(BF)
    plan = row_steps(rows)
    terms = [along_row(messages[0], plan[0])]
    terms += [along_row(m.at[B:].set(chip_weight), plan[i]) for i, m in enumerate(messages) if i > 0]
    (grad_feat,) = call(
        functools.partial(feature_kernel, rows), [slab], (place, weight, term, *terms), [pltpu.VMEM] * (rows + 2)
    )
    mine = terms[1][B:]
    swapped = across(mine)
    weights = {0: chip_weight, 2: jnp.where(even, mine, swapped), 1: jnp.where(even, swapped, mine)}
    weights.update({plan[k][0]: term[B:] for k, term in enumerate(terms) if k > 1})
    row_weight = sum_in_order([weights[step] for step in range(rows)], r, rows).astype(BF)
    first, second = depth - 2, depth - 1
    mine = along_depth(row_weight, (first, second))
    weights = {step: along_depth(row_weight, (step, step)) for step in range(1, first)}
    swapped = across(mine)
    weights.update({0: row_weight, first: jnp.where(even, mine, swapped), second: jnp.where(even, swapped, mine)})
    scale = (slab_rows * rows * cols) ** (-0.5)
    summed = sum_in_order([weights[step] for step in range(depth)], z, depth)
    grad_feat, summed = call(
        functools.partial(last_kernel, scale), [slab, jax.ShapeDtypeStruct((F, F), F32)], (grad_feat, summed), [pltpu.VMEM] * 2
    )
    return grad_feat, summed


def solution(mesh):
    placed = (
        P(("row", "col"), None),
        P(("row", "col"), None),
        P(("row", "col"), None),
        P(),
        P("row", "col", None, None, None, None),
        P("row", "col", None, None),
        P("row", "col", None),
        P(("row", "col")),
    )
    return jax.shard_map(
        shards,
        mesh=mesh,
        in_specs=placed,
        out_specs=(P(("row", "col"), None), P()),
        check_vma=False,
    )
```
